32 devices in a mesh: row: 4 (over z), col: 8 (over y, x, core).
Axes of the slice: x: 2, y: 2, z: 4, core: 2. Of those that a mesh axis runs over, the one named last changes fastest.
Arguments:
- momentum: float32 [16384, 16384], P('row', 'col'), may hold values from -18 to 18
- gradient: bfloat16 [16384, 16384], P('row', 'col'), may hold values from -6 to 6
- right_factor: float32 [16384, 64], P('col'), may hold values from -1 to 1
Outputs:
- update: bfloat16 [16384, 16384], P('row', 'col')
- left: float32 [16384, 64], P('row')
- normed: float32 [16384, 64], P('col')
- new_momentum: float32 [16384, 16384], P('row', 'col')
- first_factor: float32 [64, 64], replicated
The draws below stay inside these ranges and needn't reach their ends.
All inputs are finite; a program needn't handle non-finite values.
Results may differ from the reference program's by a relative error of at most 0.001.
Values sent between devices are 32-bit elements; how exact they have to be, the bound alone decides.
A program may use at most 192 MiB of HBM per device.

```python
import math
import jax
import jax.numpy as jnp
from jax import lax

NROW = 16384
NCOL = 16384
RANK = 64


def draw_right_factor(key, part):
    key_common = jax.random.fold_in(key, 11)
    key_own = jax.random.fold_in(key, 23)
    key_gain = jax.random.fold_in(key, 37)
    key_spread = jax.random.fold_in(key, 41)
    common = jax.random.truncated_normal(key_common, -5.0, 5.0, (NCOL,), jnp.float32)
    own = jax.random.truncated_normal(key_own, -5.0, 5.0, (NCOL, RANK), jnp.float32)
    gains = jax.random.uniform(key_gain, (RANK,), jnp.float32, 0.7, 1.3)
    spread = jnp.exp(jax.random.uniform(key_spread, (RANK,), jnp.float32, math.log(0.015), math.log(0.05)))
    raw = common[:, None] * gains[None, :] + own * spread[None, :]
    return (raw / jnp.max(jnp.abs(raw))).astype(jnp.float32)


def draw_momentum(key, part):
    key_values = jax.random.fold_in(key, 53)
    position = jnp.arange(NROW, dtype=jnp.float32) / jnp.float32(NROW)
    values = jax.random.truncated_normal(key_values, -6.0, 6.0, (NROW, NCOL), jnp.float32)
    row_scale = jnp.exp(position * math.log(3.0))
    return (values * row_scale[:, None]).astype(jnp.float32)


def level_of(rng, shape, cuts, low, largest):
    def one(axis_at, shards_of):
        heights = jax.random.uniform(jax.random.fold_in(jax.random.fold_in(rng, 6), axis_at), (shards_of,), jnp.float32, low / len(cuts), largest / len(cuts))
        return jnp.repeat(jnp.exp(heights), shape[axis_at] // shards_of).reshape((-1,) + (1,) * (len(shape) - axis_at - 1))

    gain = one(*cuts[0])
    for cut in cuts[1:]:
        gain = gain * one(*cut)
    return gain


def gaussian(own_key, shape, width, reach, shards=(), held_as=jnp.bfloat16):
    values = jax.random.normal(own_key, shape, jnp.float32) * width
    if len(shards) > 0:
        values = level_of(own_key, shape, shards, -0.22, 0.18) * values
    return jnp.clip(values, min=-reach, max=reach).astype(held_as)


def setup_inputs(seed: int = 0) -> dict:
    key_of = jax.random.split(jax.random.key(seed), 4)
    return {
        "momentum": draw_momentum(jax.random.fold_in(key_of[3], 71), 0),
        "gradient": gaussian(key_of[1], (NROW, NCOL), 1.0, 6.0, ((0, 4), (1, 8))),
        "right_factor": draw_right_factor(jax.random.fold_in(key_of[3], 71), 0),
    }


HIGH = lax.Precision.HIGHEST

def cholesky_parts(raw):
    gram = jnp.dot(raw.T.astype(jnp.float32), raw.astype(jnp.float32), precision=HIGH, preferred_element_type=jnp.float32)
    lower = jnp.linalg.cholesky(gram)
    solved = lax.linalg.triangular_solve(lower, raw, left_side=False, lower=True, transpose_a=True)
    return (solved, lower)

def reference(momentum, gradient, right_factor):
    blended = momentum + gradient.astype(jnp.float32)
    left_raw = jnp.dot(blended.astype(jnp.float32), right_factor.astype(jnp.float32), precision=HIGH, preferred_element_type=jnp.float32)
    left_one, lower_one = cholesky_parts(left_raw)
    first_factor = lower_one / jnp.sqrt(jnp.float32(NROW) * jnp.float32(NCOL))
    left, lower_two = cholesky_parts(left_one)
    right = lax.dot_general(blended.astype(jnp.float32), left.astype(jnp.float32), (((0,), (0,)), ((), ())), precision=HIGH, preferred_element_type=jnp.float32)
    norms = jnp.sqrt(lax.optimization_barrier(jnp.sum(right * right, axis=0)))
    normed = right / (norms + 1e-06)
    scale = jnp.sqrt(jnp.float32(NROW) * jnp.float32(NCOL) / jnp.float32(RANK))
    update = (scale * jnp.dot(left.astype(jnp.float32), normed.T.astype(jnp.float32), precision=HIGH, preferred_element_type=jnp.float32)).astype(jnp.bfloat16)
    new_momentum = blended - 0.05 * jnp.dot(left.astype(jnp.float32), right.T.astype(jnp.float32), precision=HIGH, preferred_element_type=jnp.float32)
    return (update, left, normed, new_momentum, first_factor)
```

```python
import functools
import math

import jax
import jax.numpy as jnp
from jax import lax
from jax.experimental import pallas as pl
from jax.experimental.pallas import tpu as pltpu
from jax.sharding import PartitionSpec as P

F32 = jnp.float32
BF16 = jnp.bfloat16
HIGH = lax.Precision.HIGHEST
SLOTS = 5
MIB = 1024 * 1024


def dot_high(a, b, dims):
    return lax.dot_general(a, b, (dims, ((), ())), precision=HIGH, preferred_element_type=F32)


def dot_bf16(a, b):
    return lax.dot_general(a, b, (((1,), (0,)), ((), ())), preferred_element_type=F32)


def halves(x):
    high = x.astype(BF16)
    return high, (x - high.astype(F32)).astype(BF16)


def eliminate(gram):
    rank = gram.shape[0]
    rows = lax.broadcasted_iota(jnp.int32, (rank, rank), 0)
    cols = lax.broadcasted_iota(jnp.int32, (rank, rank), 1)
    eye = jnp.where(rows == cols, 1.0, 0.0).astype(F32)
    wide = jnp.concatenate([gram, eye], axis=1)
    at = lax.broadcasted_iota(jnp.int32, (rank, 1), 0)
    root = jnp.zeros((rank, 1), F32)
    for j in range(rank):
        column = wide[:, j : j + 1]
        pivot = wide[j : j + 1, j : j + 1]
        row = wide[j : j + 1, :] * (1.0 / pivot)
        root = jnp.where(at == j, lax.rsqrt(pivot), root)
        wide = wide - jnp.where(at > j, column, 0.0) * row
    wide = wide * root
    upper = jnp.where(cols >= rows, wide[:, :rank], 0.0)
    return upper, wide[:, rank:]


class Exchange:
    def __init__(self, axis, count, local, slots, send, recv):
        self.axis, self.count = axis, count
        self.local, self.slots, self.send, self.recv = local, slots, send, recv
        self.me = lax.axis_index(axis)

    def copy(self, step, peer, slot):
        return pltpu.make_async_remote_copy(
            src_ref=self.local,
            dst_ref=self.slots.at[slot],
            send_sem=self.send.at[step],
            recv_sem=self.recv.at[slot],
            device_id={self.axis: peer},
            device_id_type=pl.DeviceIdType.MESH,
        )

    def start(self, value):
        self.local[...] = value
        self.slots[self.me] = value
        for step in range(1, self.count):
            self.copy(step, lax.rem(self.me + step, self.count), self.me).start()

    def finish(self):
        for step in range(1, self.count):
            peer = lax.rem(self.me + step, self.count)
            self.copy(step, peer, peer).wait()
        total = self.slots[0]
        for step in range(1, self.count):
            total = total + self.slots[step]
        return total


class AllReduce:
    def __init__(self, axis, count, rank, acc, full, boxes, send, recv):
        self.axis, self.acc, self.full, self.boxes = axis, acc, full, boxes
        self.send, self.recv = send, recv
        me = lax.axis_index(axis)
        offset, size = 0, rank
        self.stages = []
        for bit in range(count.bit_length() - 1):
            one = lax.rem(me // (1 << bit), 2)
            peer = me + (1 - 2 * one) * (1 << bit)
            halve = size >= 16
            if halve:
                half = size // 2
                keep, give = offset + one * half, offset + (1 - one) * half
            else:
                half, keep, give = size, offset, offset
            self.stages.append((peer, halve, half, keep, give))
            offset, size = keep, half
        self.offset, self.size = offset, size
        self.back = [s for s in reversed(range(len(self.stages))) if self.stages[s][1]]
        self.steps = len(self.stages) + len(self.back)

    def rows(self, start, size):
        return pl.ds(start if isinstance(start, int) else pl.multiple_of(start, 8), size)

    def copy(self, step, block, cols):
        n = len(self.stages)
        if step < n:
            peer, halve, half, keep, give = self.stages[step]
            src = self.acc.at[self.rows(give, half), cols]
            dst = self.boxes[step].at[:, cols]
        else:
            peer, halve, half, keep, give = self.stages[self.back[step - n]]
            src = self.full.at[self.rows(keep, half), cols]
            dst = self.full.at[self.rows(keep, half), cols]
        return pltpu.make_async_remote_copy(
            src_ref=src,
            dst_ref=dst,
            send_sem=self.send.at[step, block],
            recv_sem=self.recv.at[step, block],
            device_id={self.axis: peer},
            device_id_type=pl.DeviceIdType.MESH,
        )

    def start(self, step, block, cols):
        self.copy(step, block, cols).start()

    def finish(self, step, block, cols):
        self.copy(step, block, cols).wait()
        n = len(self.stages)
        if step < n:
            half, keep = self.stages[step][2:4]
            kept = self.rows(keep, half)
            self.acc[kept, cols] = self.acc[kept, cols] + self.boxes[step][:, cols]
            if step == n - 1:
                own = self.rows(self.offset, self.size)
                self.full[own, cols] = self.acc[own, cols]
        if step + 1 < self.steps:
            self.start(step + 1, block, cols)


def box_rows(count, rank):
    sizes, size = [], rank
    for _ in range(count.bit_length() - 1):
        if size >= 16:
            size //= 2
        sizes.append(size)
    return sizes


def step_count(count, rank):
    size, steps = rank, 0
    for _ in range(count.bit_length() - 1):
        steps += 1
        if size >= 16:
            size //= 2
            steps += 1
    return steps


def factor_kernel(plan, mom, grad, rf, yt, linv, rt, nt, first, *refs):
    m, n, rank, nr, nc, tile, chunk, group = plan
    refs = list(refs)
    take = lambda count: [refs.pop(0) for _ in range(count)]
    (bh, bm, mbuf, gbuf, rp, acc, full, yp, wacc, wfull, qs, us) = take(12)
    boxes_y = take(nc.bit_length() - 1)
    boxes_w = take(nr.bit_length() - 1)
    ex = [take(4) for _ in range(3)]
    (in_sem, ysend, yrecv, wsend, wrecv) = take(5)

    tiles, chunks, per = m // tile, m // chunk, chunk // tile
    slots = min(SLOTS, tiles)

    def load(t, slot):
        src = pl.ds(pl.multiple_of(t * tile, tile), tile)
        return (
            pltpu.make_async_copy(mom.at[src, :], mbuf.at[slot], in_sem.at[0, slot]),
            pltpu.make_async_copy(grad.at[src, :], gbuf.at[slot], in_sem.at[1, slot]),
        )

    for t in range(slots):
        for c in load(t, t):
            c.start()

    barrier = pltpu.get_barrier_semaphore()
    row, col = lax.axis_index("row"), lax.axis_index("col")
    for step in range(1, nc):
        pl.semaphore_signal(
            barrier, inc=1, device_id={"col": lax.rem(col + step, nc)}, device_id_type=pl.DeviceIdType.MESH
        )
    for step in range(1, nr):
        pl.semaphore_signal(
            barrier, inc=1, device_id={"row": lax.rem(row + step, nr)}, device_id_type=pl.DeviceIdType.MESH
        )

    r = rf[...]
    r_high, r_rest = halves(r)
    r_mid, r_low = halves(r - r_high.astype(F32))
    rp[:, :rank] = r_high
    rp[:, rank : 2 * rank] = r_mid
    rp[:, 2 * rank :] = r_low
    gram_r = dot_high(r, r, ((0,), (0,)))

    pl.semaphore_wait(barrier, nc + nr - 2)

    ex_r = Exchange("col", nc, *ex[0])
    ex_g = Exchange("row", nr, *ex[1])
    ex_s = Exchange("col", nc, *ex[2])
    sum_y = AllReduce("col", nc, rank, acc, full, boxes_y, ysend, yrecv)
    sum_w = AllReduce("row", nr, rank, wacc, wfull, boxes_w, wsend, wrecv)

    ex_r.start(gram_r)

    def chunk_cols(c):
        return pl.ds(pl.multiple_of(c * chunk, chunk), chunk)

    def body(c, carry):
        for step in reversed(range(sum_y.steps)):
            old = c - step - 1

            @pl.when((old >= 0) & (old < chunks))
            def _(step=step, old=old):
                sum_y.finish(step, old, chunk_cols(old))

        @pl.when(c < chunks)
        def _():
            for k in range(per):
                t = c * per + k
                slot = lax.rem(t, slots)
                for copy in load(t, slot):
                    copy.wait()
                blended = mbuf[slot] + gbuf[slot].astype(F32)
                high, low = halves(blended)
                here = pl.ds(pl.multiple_of(t * tile, tile), tile)
                bh[here, :] = high
                bm[here, :] = low
                part = dot_bf16(high, rp[...]) + dot_bf16(low, rp[...])
                part = part.T
                part = part[:rank] + (part[rank : 2 * rank] + part[2 * rank :])
                acc[:, here] = part

                @pl.when(t + slots < tiles)
                def _():
                    for copy in load(t + slots, slot):
                        copy.start()

            sum_y.start(0, c, chunk_cols(c))

        @pl.when(c == min(2, chunks - 1))
        def _():
            g = ex_r.finish()
            rows = lax.broadcasted_iota(jnp.int32, (rank, rank), 0)
            cols = lax.broadcasted_iota(jnp.int32, (rank, rank), 1)
            diag = jnp.where(rows == cols, g, 0.0)
            trace = jnp.sum(jnp.sum(diag, axis=1, keepdims=True), axis=0, keepdims=True)
            g = g + jnp.where(rows == cols, trace * (2.0**-22), 0.0)
            upper, inverse = eliminate(g)
            us[...] = upper
            qs[...] = inverse

        return carry

    lax.fori_loop(0, chunks + sum_y.steps, body, 0)

    q = qs[...]

    def whiten(c, gram):
        cols = chunk_cols(c)
        y = dot_high(q, full[:, cols], ((1,), (0,)))
        yt[:, cols] = y
        high, low = halves(y)
        yp[:rank, cols] = high
        yp[rank:, cols] = low
        return gram + dot_high(y, y, ((1,), (1,)))

    gram_y = lax.fori_loop(0, chunks, whiten, jnp.zeros((rank, rank), F32))
    ex_g.start(gram_y)

    groups = n // group
    sub = min(256, group)

    def group_cols(g):
        return pl.ds(g * group, group)

    for g in range(groups):

        def right_part(s, carry):
            cols = pl.ds(pl.multiple_of(g * group + s * sub, sub), sub)
            w = dot_bf16(yp[...], bh[:, cols]) + dot_bf16(yp[...], bm[:, cols])
            wacc[:, cols] = w[:rank] + w[rank:]
            return carry

        lax.fori_loop(0, group // sub, right_part, 0)
        sum_w.start(0, g, group_cols(g))

    g_all = ex_g.finish()
    upper, inverse = eliminate(g_all)
    first[...] = dot_high(us[...], upper, ((0,), (1,))) * (1.0 / math.sqrt(float(m * nr) * float(n * nc)))
    for g in range(groups):
        sum_w.finish(0, g, group_cols(g))
    g_two = dot_high(dot_high(inverse, g_all, ((1,), (0,))), inverse, ((1,), (1,)))
    _, inverse_two = eliminate(g_two)
    both = dot_high(inverse_two, inverse, ((1,), (0,)))
    linv[...] = both
    for step in range(1, sum_w.steps):
        for g in range(groups):
            sum_w.finish(step, g, group_cols(g))
    squares = jnp.zeros((rank, 1), F32)
    for g in range(groups):
        right = dot_high(both, wfull[:, group_cols(g)], ((1,), (0,)))
        rt[:, group_cols(g)] = right
        squares = squares + jnp.sum(right * right, axis=1, keepdims=True)
    ex_s.start(jnp.broadcast_to(squares, (rank, 128)))
    norms = jnp.sqrt(ex_s.finish()[:, :1]) + 1e-06
    nt[...] = rt[...] * (1.0 / norms)


def factors(plan, momentum, gradient, right_factor):
    m, n, rank, nr, nc, tile, chunk, group = plan
    slots = min(SLOTS, m // tile)
    vmem = pltpu.VMEM
    dma = pltpu.SemaphoreType.DMA

    def exchange(count, width):
        return [vmem((rank, width), F32), vmem((count, rank, width), F32), dma((count,)), dma((count,))]

    scratch = [
        vmem((m, n), BF16),
        vmem((m, n), BF16),
        vmem((slots, tile, n), F32),
        vmem((slots, tile, n), BF16),
        vmem((n, 3 * rank), BF16),
        vmem((rank, m), F32),
        vmem((rank, m), F32),
        vmem((2 * rank, m), BF16),
        vmem((rank, n), F32),
        vmem((rank, n), F32),
        vmem((rank, rank), F32),
        vmem((rank, rank), F32),
    ]
    scratch += [vmem((rows, m), F32) for rows in box_rows(nc, rank)]
    scratch += [vmem((rows, n), F32) for rows in box_rows(nr, rank)]
    scratch += exchange(nc, rank) + exchange(nr, rank) + exchange(nc, 128)
    steps_y, steps_w = step_count(nc, rank), step_count(nr, rank)
    scratch += [
        dma((2, slots)),
        dma((steps_y, m // chunk)),
        dma((steps_y, m // chunk)),
        dma((steps_w, n // group)),
        dma((steps_w, n // group)),
    ]
    whole = pl.BlockSpec(memory_space=vmem)
    return pl.pallas_call(
        functools.partial(factor_kernel, plan),
        out_shape=[
            jax.ShapeDtypeStruct((rank, m), F32),
            jax.ShapeDtypeStruct((rank, rank), F32),
            jax.ShapeDtypeStruct((rank, n), F32),
            jax.ShapeDtypeStruct((rank, n), F32),
            jax.ShapeDtypeStruct((rank, rank), F32),
        ],
        in_specs=[pl.BlockSpec(memory_space=pl.ANY), pl.BlockSpec(memory_space=pl.ANY), whole],
        out_specs=[whole] * 5,
        scratch_shapes=scratch,
        compiler_params=pltpu.CompilerParams(
            collective_id=0, has_side_effects=True, vmem_limit_bytes=60 * MIB
        ),
        name="factors",
    )(momentum, gradient, right_factor)


def output_kernel(scale, rank, mom, grad, yt, linv, rt, nt, first, update, left, normed, new, first_out, rhs_u, rhs_m):
    @pl.when(pl.program_id(0) == 0)
    def _():
        normed_t = nt[...]
        normed[...] = normed_t.T
        first_out[...] = first[...]
        for ref, value in ((rhs_u, normed_t * scale), (rhs_m, rt[...] * 0.05)):
            high, low = halves(value)
            for k in range(2):
                ref[2 * k * rank : (2 * k + 1) * rank, :] = high
                ref[(2 * k + 1) * rank : (2 * k + 2) * rank, :] = low

    lt = dot_high(linv[...], yt[...], ((1,), (0,)))
    left[...] = lt.T
    high = lt.astype(BF16).astype(F32)
    low = lt - high
    lhs = jnp.concatenate([high, high, low, low], axis=0).T.astype(BF16)
    update[...] = dot_bf16(lhs, rhs_u[...]).astype(BF16)
    new[...] = (mom[...] + grad[...].astype(F32)) - dot_bf16(lhs, rhs_m[...])


def outputs(scale, tile, momentum, gradient, yt, linv, rt, nt, first):
    m, n = momentum.shape
    rank = linv.shape[0]
    fixed = lambda shape: pl.BlockSpec(shape, lambda i: (0, 0))
    rows = lambda width: pl.BlockSpec((tile, width), lambda i: (i, 0))
    return pl.pallas_call(
        functools.partial(output_kernel, scale, rank),
        grid=(m // tile,),
        out_shape=[
            jax.ShapeDtypeStruct((m, n), BF16),
            jax.ShapeDtypeStruct((m, rank), F32),
            jax.ShapeDtypeStruct((n, rank), F32),
            jax.ShapeDtypeStruct((m, n), F32),
            jax.ShapeDtypeStruct((rank, rank), F32),
        ],
        in_specs=[
            rows(n),
            rows(n),
            pl.BlockSpec((rank, tile), lambda i: (0, i)),
            fixed((rank, rank)),
            fixed((rank, n)),
            fixed((rank, n)),
            fixed((rank, rank)),
        ],
        out_specs=[rows(n), rows(rank), fixed((n, rank)), rows(n), fixed((rank, rank))],
        scratch_shapes=[pltpu.VMEM((4 * rank, n), BF16), pltpu.VMEM((4 * rank, n), BF16)],
        compiler_params=pltpu.CompilerParams(vmem_limit_bytes=40 * MIB),
        name="outputs",
    )(momentum, gradient, yt, linv, rt, nt, first)


def on_device(nr, nc, momentum, gradient, right_factor):
    m, n = momentum.shape
    rank = right_factor.shape[1]
    tile = min(128, m)
    chunk = min(512, m)
    group = min(1024, n)
    plan = (m, n, rank, nr, nc, tile, chunk, group)
    scale = math.sqrt(float(m * nr) * float(n * nc) / float(rank))
    yt, linv, rt, nt, first = factors(plan, momentum, gradient, right_factor)
    return tuple(outputs(scale, tile, momentum, gradient, yt, linv, rt, nt, first))


def solution(mesh):
    in_specs = (P("row", "col"), P("row", "col"), P("col", None))
    out_specs = (P("row", "col"), P("row", None), P("col", None), P("row", "col"), P())
    return jax.shard_map(
        functools.partial(on_device, mesh.shape["row"], mesh.shape["col"]),
        mesh=mesh,
        in_specs=in_specs,
        out_specs=out_specs,
        check_vma=False,
    )
```

```python
import functools
import math

import jax
import jax.numpy as jnp
from jax import lax
from jax.experimental import pallas as pl
from jax.experimental.pallas import tpu as pltpu
from jax.sharding import PartitionSpec as P

F32 = jnp.float32
BF16 = jnp.bfloat16
HIGH = lax.Precision.HIGHEST
SLOTS = 5
MIB = 1024 * 1024


def dot_high(a, b, dims):
    return lax.dot_general(a, b, (dims, ((), ())), precision=HIGH, preferred_element_type=F32)


def dot_bf16(a, b):
    return lax.dot_general(a, b, (((1,), (0,)), ((), ())), preferred_element_type=F32)


def halves(x):
    high = x.astype(BF16)
    return high, (x - high.astype(F32)).astype(BF16)


def widen(gram):
    rank = gram.shape[0]
    rows = lax.broadcasted_iota(jnp.int32, (rank, rank), 0)
    cols = lax.broadcasted_iota(jnp.int32, (rank, rank), 1)
    return jnp.concatenate([gram, jnp.where(rows == cols, 1.0, 0.0).astype(F32)], axis=1)


def eliminate_columns(wide, root, columns):
    at = lax.broadcasted_iota(jnp.int32, (wide.shape[0], 1), 0)
    for j in columns:
        column = wide[:, j : j + 1]
        pivot = wide[j : j + 1, j : j + 1]
        row = wide[j : j + 1, :] * (1.0 / pivot)
        root = jnp.where(at == j, lax.rsqrt(pivot), root)
        wide = wide - jnp.where(at > j, column, 0.0) * row
    return wide, root


def split_factors(wide, root):
    rank = wide.shape[0]
    rows = lax.broadcasted_iota(jnp.int32, (rank, rank), 0)
    cols = lax.broadcasted_iota(jnp.int32, (rank, rank), 1)
    wide = wide * root
    return jnp.where(cols >= rows, wide[:, :rank], 0.0), wide[:, rank:]


def eliminate(gram):
    rank = gram.shape[0]
    return split_factors(*eliminate_columns(widen(gram), jnp.zeros((rank, 1), F32), range(rank)))


class Exchange:
    def __init__(self, axis, count, local, slots, send, recv):
        self.axis, self.count = axis, count
        self.local, self.slots, self.send, self.recv = local, slots, send, recv
        self.me = lax.axis_index(axis)

    def copy(self, step, peer, slot):
        return pltpu.make_async_remote_copy(
            src_ref=self.local,
            dst_ref=self.slots.at[slot],
            send_sem=self.send.at[step],
            recv_sem=self.recv.at[slot],
            device_id={self.axis: peer},
            device_id_type=pl.DeviceIdType.MESH,
        )

    def start(self, value):
        self.local[...] = value
        self.slots[self.me] = value
        for step in range(1, self.count):
            self.copy(step, lax.rem(self.me + step, self.count), self.me).start()

    def finish(self):
        for step in range(1, self.count):
            peer = lax.rem(self.me + step, self.count)
            self.copy(step, peer, peer).wait()
        total = self.slots[0]
        for step in range(1, self.count):
            total = total + self.slots[step]
        return total


class AllReduce:
    def __init__(self, axis, count, rank, acc, full, boxes, send, recv):
        self.axis, self.acc, self.full, self.boxes = axis, acc, full, boxes
        self.send, self.recv = send, recv
        me = lax.axis_index(axis)
        offset, size = 0, rank
        self.stages = []
        for bit in range(count.bit_length() - 1):
            one = lax.rem(me // (1 << bit), 2)
            peer = me + (1 - 2 * one) * (1 << bit)
            halve = size >= 16
            if halve:
                half = size // 2
                keep, give = offset + one * half, offset + (1 - one) * half
            else:
                half, keep, give = size, offset, offset
            self.stages.append((peer, halve, half, keep, give))
            offset, size = keep, half
        self.offset, self.size = offset, size
        self.back = [s for s in reversed(range(len(self.stages))) if self.stages[s][1]]
        self.steps = len(self.stages) + len(self.back)

    def rows(self, start, size):
        return pl.ds(start if isinstance(start, int) else pl.multiple_of(start, 8), size)

    def copy(self, step, block, cols):
        n = len(self.stages)
        if step < n:
            peer, halve, half, keep, give = self.stages[step]
            src = self.acc.at[self.rows(give, half), cols]
            dst = self.boxes[step].at[:, cols]
        else:
            peer, halve, half, keep, give = self.stages[self.back[step - n]]
            src = self.full.at[self.rows(keep, half), cols]
            dst = self.full.at[self.rows(keep, half), cols]
        return pltpu.make_async_remote_copy(
            src_ref=src,
            dst_ref=dst,
            send_sem=self.send.at[step, block],
            recv_sem=self.recv.at[step, block],
            device_id={self.axis: peer},
            device_id_type=pl.DeviceIdType.MESH,
        )

    def start(self, step, block, cols):
        self.copy(step, block, cols).start()

    def finish(self, step, block, cols):
        self.copy(step, block, cols).wait()
        n = len(self.stages)
        if step < n:
            half, keep = self.stages[step][2:4]
            kept = self.rows(keep, half)
            self.acc[kept, cols] = self.acc[kept, cols] + self.boxes[step][:, cols]
            if step == n - 1:
                own = self.rows(self.offset, self.size)
                self.full[own, cols] = self.acc[own, cols]
        if step + 1 < self.steps:
            self.start(step + 1, block, cols)


def box_rows(count, rank):
    sizes, size = [], rank
    for _ in range(count.bit_length() - 1):
        if size >= 16:
            size //= 2
        sizes.append(size)
    return sizes


def step_count(count, rank):
    size, steps = rank, 0
    for _ in range(count.bit_length() - 1):
        steps += 1
        if size >= 16:
            size //= 2
            steps += 1
    return steps


def factor_kernel(plan, mom, grad, rf, lhs, lt, rt, nt, first, *refs):
    m, n, rank, nr, nc, tile, chunk, group = plan
    refs = list(refs)
    take = lambda count: [refs.pop(0) for _ in range(count)]
    (bh, bm, mbuf, gbuf, rp, acc, full, yp, ws, rs) = take(10)
    boxes_y = take(nc.bit_length() - 1)
    boxes_w = take(nr.bit_length() - 1)
    ex = [take(4) for _ in range(3)]
    (in_sem, ysend, yrecv, wsend, wrecv) = take(5)

    tiles, chunks, per = m // tile, m // chunk, chunk // tile
    pair = min(2, per)
    slots = min(SLOTS, tiles)

    def load(t, slot):
        src = pl.ds(pl.multiple_of(t * tile, tile), tile)
        return (
            pltpu.make_async_copy(mom.at[src, :], mbuf.at[slot], in_sem.at[0, slot]),
            pltpu.make_async_copy(grad.at[src, :], gbuf.at[slot], in_sem.at[1, slot]),
        )

    for t in range(slots):
        for c in load(t, t):
            c.start()

    barrier = pltpu.get_barrier_semaphore()
    row, col = lax.axis_index("row"), lax.axis_index("col")
    for step in range(1, nc):
        pl.semaphore_signal(
            barrier, inc=1, device_id={"col": lax.rem(col + step, nc)}, device_id_type=pl.DeviceIdType.MESH
        )
    for step in range(1, nr):
        pl.semaphore_signal(
            barrier, inc=1, device_id={"row": lax.rem(row + step, nr)}, device_id_type=pl.DeviceIdType.MESH
        )

    r = rf[...]
    r_high, r_rest = halves(r)
    r_mid, r_low = halves(r - r_high.astype(F32))
    pieces = jnp.concatenate([p.astype(F32) for p in (r_high, r_mid, r_low)], axis=0)
    rp[...] = pieces.T.astype(BF16)
    gram_r = dot_high(r, r, ((1,), (1,)))

    pl.semaphore_wait(barrier, nc + nr - 2)

    ex_r = Exchange("col", nc, *ex[0])
    ex_g = Exchange("row", nr, *ex[1])
    ex_s = Exchange("col", nc, *ex[2])
    sum_y = AllReduce("col", nc, rank, acc, full, boxes_y, ysend, yrecv)
    sum_w = AllReduce("row", nr, rank, acc, full, boxes_w, wsend, wrecv)

    ex_r.start(gram_r)

    def chunk_cols(c):
        return pl.ds(pl.multiple_of(c * chunk, chunk), chunk)

    def body(c, carry):
        for step in reversed(range(sum_y.steps)):
            old = c - step - 1

            @pl.when((old >= 0) & (old < chunks))
            def _(step=step, old=old):
                sum_y.finish(step, old, chunk_cols(old))

        @pl.when(c < chunks)
        def _():
            for k in range(0, per, pair):
                for t in range(pair):
                    t = c * per + k + t
                    slot = lax.rem(t, slots)
                    for copy in load(t, slot):
                        copy.wait()
                    high, low = halves(mbuf[slot] + gbuf[slot].astype(F32))
                    here = pl.ds(pl.multiple_of(t * tile, tile), tile)
                    bh[here, :] = high
                    bm[here, :] = low

                    @pl.when(t + slots < tiles)
                    def _(t=t, slot=slot):
                        for copy in load(t + slots, slot):
                            copy.start()

                here = pl.ds(pl.multiple_of((c * per + k) * tile, pair * tile), pair * tile)
                both = jnp.concatenate([bh[here, :], bm[here, :]], axis=0)
                part = dot_bf16(both, rp[...])
                part = (part[: pair * tile] + part[pair * tile :]).T
                acc[:, here] = part[:rank] + (part[rank : 2 * rank] + part[2 * rank :])

            sum_y.start(0, c, chunk_cols(c))

        @pl.when(c == chunks)
        def _():
            g = ex_r.finish()
            rows = lax.broadcasted_iota(jnp.int32, (rank, rank), 0)
            cols = lax.broadcasted_iota(jnp.int32, (rank, rank), 1)
            diag = jnp.where(rows == cols, g, 0.0)
            trace = jnp.sum(jnp.sum(diag, axis=1, keepdims=True), axis=0, keepdims=True)
            ws[...] = widen(g + jnp.where(rows == cols, trace * (2.0**-22), 0.0))
            rs[...] = jnp.zeros((rank, 1), F32)

        for k in range(4):

            @pl.when(c == chunks + min(k, sum_y.steps - 1))
            def _(k=k):
                wide, root = eliminate_columns(
                    ws[...], rs[...], range(k * rank // 4, (k + 1) * rank // 4)
                )
                ws[...] = wide
                rs[...] = root

        return carry

    lax.fori_loop(0, chunks + sum_y.steps, body, 0)
    upper_r, q = split_factors(ws[...], rs[...])

    def whiten(c, gram):
        cols = chunk_cols(c)
        y = dot_high(q, full[:, cols], ((1,), (0,)))
        lt[:, cols] = y
        high, low = halves(y)
        yp[:rank, cols] = high
        yp[rank:, cols] = low
        return gram + dot_high(y, y, ((1,), (1,)))

    gram_y = lax.fori_loop(0, chunks, whiten, jnp.zeros((rank, rank), F32))
    ex_g.start(gram_y)

    groups = n // group
    sub = min(256, group)

    def group_cols(g):
        return pl.ds(g * group, group)

    def right_part(g):
        def one(s, carry):
            cols = pl.ds(pl.multiple_of(g * group + s * sub, sub), sub)
            w = dot_bf16(yp[...], bh[:, cols]) + dot_bf16(yp[...], bm[:, cols])
            acc[:, cols] = w[:rank] + w[rank:]
            return carry

        lax.fori_loop(0, group // sub, one, 0)
        sum_w.start(0, g, group_cols(g))

    def left_part(c, carry):
        cols = chunk_cols(c)
        left_t = dot_high(both, lt[:, cols], ((1,), (0,)))
        lt[:, cols] = left_t
        high = left_t.astype(BF16).astype(F32)
        low = left_t - high
        lhs[cols, :] = jnp.concatenate([high, high, low, low], axis=0).T.astype(BF16)
        return carry

    for i in range(groups + max(sum_w.steps, 3)):
        for step in reversed(range(sum_w.steps)):
            if 0 <= i - 1 - step < groups:
                sum_w.finish(step, i - 1 - step, group_cols(i - 1 - step))
        if i < groups:
            right_part(i)
        if i == groups:
            g_all = ex_g.finish()
            upper, inverse = eliminate(g_all)
            first[...] = dot_high(upper_r, upper, ((0,), (1,))) * (
                1.0 / math.sqrt(float(m * nr) * float(n * nc))
            )
        if i == groups + 1:
            g_two = dot_high(dot_high(inverse, g_all, ((1,), (0,))), inverse, ((1,), (1,)))
            _, inverse_two = eliminate(g_two)
            both = dot_high(inverse_two, inverse, ((1,), (0,)))
        if i == groups + 2:
            lax.fori_loop(0, chunks, left_part, 0)

    squares = jnp.zeros((rank, 1), F32)
    for g in range(groups):
        right = dot_high(both, full[:, group_cols(g)], ((1,), (0,)))
        rt[:, group_cols(g)] = right
        squares = squares + jnp.sum(right * right, axis=1, keepdims=True)
    ex_s.start(jnp.broadcast_to(squares, (rank, 128)))
    norms = jnp.sqrt(ex_s.finish()[:, :1]) + 1e-06
    nt[...] = rt[...] * (1.0 / norms)


def factors(plan, momentum, gradient, right_factor):
    m, n, rank, nr, nc, tile, chunk, group = plan
    slots = min(SLOTS, m // tile)
    vmem = pltpu.VMEM
    dma = pltpu.SemaphoreType.DMA

    def exchange(count, width):
        return [vmem((rank, width), F32), vmem((count, rank, width), F32), dma((count,)), dma((count,))]

    scratch = [
        vmem((m, n), BF16),
        vmem((m, n), BF16),
        vmem((slots, tile, n), F32),
        vmem((slots, tile, n), BF16),
        vmem((n, 3 * rank), BF16),
        vmem((rank, max(m, n)), F32),
        vmem((rank, max(m, n)), F32),
        vmem((2 * rank, m), BF16),
        vmem((rank, 2 * rank), F32),
        vmem((rank, 1), F32),
    ]
    scratch += [vmem((rows, m), F32) for rows in box_rows(nc, rank)]
    scratch += [vmem((rows, n), F32) for rows in box_rows(nr, rank)]
    scratch += exchange(nc, rank) + exchange(nr, rank) + exchange(nc, 128)
    steps_y, steps_w = step_count(nc, rank), step_count(nr, rank)
    scratch += [
        dma((2, slots)),
        dma((steps_y, m // chunk)),
        dma((steps_y, m // chunk)),
        dma((steps_w, n // group)),
        dma((steps_w, n // group)),
    ]
    whole = pl.BlockSpec(memory_space=vmem)
    return pl.pallas_call(
        functools.partial(factor_kernel, plan),
        out_shape=[
            jax.ShapeDtypeStruct((m, 4 * rank), BF16),
            jax.ShapeDtypeStruct((rank, m), F32),
            jax.ShapeDtypeStruct((rank, n), F32),
            jax.ShapeDtypeStruct((rank, n), F32),
            jax.ShapeDtypeStruct((rank, rank), F32),
        ],
        in_specs=[pl.BlockSpec(memory_space=pl.ANY), pl.BlockSpec(memory_space=pl.ANY), whole],
        out_specs=[whole] * 5,
        scratch_shapes=scratch,
        compiler_params=pltpu.CompilerParams(
            collective_id=0, has_side_effects=True, vmem_limit_bytes=60 * MIB
        ),
        name="factors",
    )(momentum, gradient, right_factor)


def output_kernel(scale, rank, mom, grad, lhs, lt, rt, nt, first, update, left, normed, new, first_out, rhs_u, rhs_m):
    tile, n = mom.shape

    @pl.when(pl.program_id(0) == 0)
    def _():
        normed[...] = nt[...]
        first_out[...] = first[...]
        for ref, value in ((rhs_u, nt[...] * scale), (rhs_m, rt[...] * 0.05)):
            high, low = halves(value)
            for k in range(2):
                ref[2 * k * rank : (2 * k + 1) * rank, :] = high
                ref[(2 * k + 1) * rank : (2 * k + 2) * rank, :] = low

    here = pl.ds(pl.multiple_of(pl.program_id(0) * tile, tile), tile)
    left[...] = lt[:, here]
    rows = lhs[here, :]
    width = min(256, n)
    for at in range(0, n, width):
        cols = pl.ds(at, width)
        update[:, cols] = dot_bf16(rows, rhs_u[:, cols]).astype(BF16)
        new[:, cols] = (mom[:, cols] + grad[:, cols].astype(F32)) - dot_bf16(rows, rhs_m[:, cols])


def outputs(scale, tile, momentum, gradient, lhs, lt, rt, nt, first):
    m, n = momentum.shape
    rank = lt.shape[0]
    fixed = lambda shape: pl.BlockSpec(shape, lambda i: (0, 0))
    rows = lambda width: pl.BlockSpec((tile, width), lambda i: (i, 0))
    whole = pl.BlockSpec(memory_space=pltpu.VMEM)
    return pl.pallas_call(
        functools.partial(output_kernel, scale, rank),
        grid=(m // tile,),
        out_shape=[
            jax.ShapeDtypeStruct((m, n), BF16),
            jax.ShapeDtypeStruct((rank, m), F32),
            jax.ShapeDtypeStruct((rank, n), F32),
            jax.ShapeDtypeStruct((m, n), F32),
            jax.ShapeDtypeStruct((rank, rank), F32),
        ],
        in_specs=[rows(n), rows(n)] + [whole] * 5,
        out_specs=[
            rows(n),
            pl.BlockSpec((rank, tile), lambda i: (0, i)),
            fixed((rank, n)),
            rows(n),
            fixed((rank, rank)),
        ],
        scratch_shapes=[pltpu.VMEM((4 * rank, n), BF16), pltpu.VMEM((4 * rank, n), BF16)],
        compiler_params=pltpu.CompilerParams(vmem_limit_bytes=40 * MIB),
        name="outputs",
    )(momentum, gradient, lhs, lt, rt, nt, first)


def on_device(nr, nc, momentum, gradient, right_factor):
    m, n = momentum.shape
    rank = right_factor.shape[1]
    tile = min(128, m)
    chunk = min(512, m)
    group = min(512, n)
    plan = (m, n, rank, nr, nc, tile, chunk, group)
    scale = math.sqrt(float(m * nr) * float(n * nc) / float(rank))
    lhs, lt, rt, nt, first = factors(plan, momentum, gradient, right_factor.T)
    update, left, normed, new, first = outputs(
        scale, min(256, m), momentum, gradient, lhs, lt, rt, nt, first
    )
    return update, left.T, normed.T, new, first


def solution(mesh):
    in_specs = (P("row", "col"), P("row", "col"), P("col", None))
    out_specs = (P("row", "col"), P("row", None), P("col", None), P("row", "col"), P())
    return jax.shard_map(
        functools.partial(on_device, mesh.shape["row"], mesh.shape["col"]),
        mesh=mesh,
        in_specs=in_specs,
        out_specs=out_specs,
        check_vma=False,
    )
```

```python
import functools
import math

import jax
import jax.numpy as jnp
from jax import lax
from jax.experimental import pallas as pl
from jax.experimental.pallas import tpu as pltpu
from jax.sharding import PartitionSpec as P

F32 = jnp.float32
BF16 = jnp.bfloat16
HIGH = lax.Precision.HIGHEST
SLOTS = 5
MIB = 1024 * 1024


def dot_high(a, b, dims):
    return lax.dot_general(a, b, (dims, ((), ())), precision=HIGH, preferred_element_type=F32)


def dot_bf16(a, b):
    return lax.dot_general(a, b, (((1,), (0,)), ((), ())), preferred_element_type=F32)


def halves(x):
    high = x.astype(BF16)
    return high, (x - high.astype(F32)).astype(BF16)


def widen(gram):
    rank = gram.shape[0]
    rows = lax.broadcasted_iota(jnp.int32, (rank, rank), 0)
    cols = lax.broadcasted_iota(jnp.int32, (rank, rank), 1)
    return jnp.concatenate([gram, jnp.where(rows == cols, 1.0, 0.0).astype(F32)], axis=1)


def eliminate_columns(wide, columns):
    rank, lanes = wide.shape
    at = lax.broadcasted_iota(jnp.int32, (8, lanes), 0)
    blocks = [wide[k : k + 8, :] for k in range(0, rank, 8)]
    for j in range(columns[0], columns[-1] + 1, 4):
        top = j // 8
        spread = [
            {k: jnp.broadcast_to(blocks[k][:, j + a : j + a + 1], (8, lanes)) for k in range(top, rank // 8)}
            for a in range(4)
        ]
        for a in range(4):
            here = j + a - 8 * top
            inverse = 1.0 / spread[a][top][here : here + 1, :]
            lows = dict(spread[a])
            lows[top] = jnp.where(at > here, lows[top], 0.0)
            for b in range(a + 1, 4):
                entry = spread[b][top][here : here + 1, :] * inverse
                spread[b] = {k: spread[b][k] - lows[k] * entry for k in lows}
            row = blocks[top][here : here + 1, :] * inverse
            for k in lows:
                blocks[k] = blocks[k] - lows[k] * row
    return jnp.concatenate(blocks, axis=0)


def split_factors(wide):
    rank = wide.shape[0]
    rows = lax.broadcasted_iota(jnp.int32, (rank, rank), 0)
    cols = lax.broadcasted_iota(jnp.int32, (rank, rank), 1)
    pivots = jnp.sum(jnp.where(rows == cols, wide[:, :rank], 0.0), axis=1, keepdims=True)
    wide = wide * (1.0 / jnp.sqrt(pivots))
    return jnp.where(cols >= rows, wide[:, :rank], 0.0), wide[:, rank:]


def eliminate(gram):
    return split_factors(eliminate_columns(widen(gram), range(gram.shape[0])))


class Exchange:
    def __init__(self, axis, count, local, slots, send, recv):
        self.axis, self.count = axis, count
        self.local, self.slots, self.send, self.recv = local, slots, send, recv
        self.me = lax.axis_index(axis)

    def copy(self, step, peer, slot):
        return pltpu.make_async_remote_copy(
            src_ref=self.local,
            dst_ref=self.slots.at[slot],
            send_sem=self.send.at[step],
            recv_sem=self.recv.at[slot],
            device_id={self.axis: peer},
            device_id_type=pl.DeviceIdType.MESH,
        )

    def start(self, value):
        self.local[...] = value
        self.slots[self.me] = value
        for step in range(1, self.count):
            self.copy(step, lax.rem(self.me + step, self.count), self.me).start()

    def finish(self):
        for step in range(1, self.count):
            peer = lax.rem(self.me + step, self.count)
            self.copy(step, peer, peer).wait()
        total = self.slots[0]
        for step in range(1, self.count):
            total = total + self.slots[step]
        return total


class AllReduce:
    def __init__(self, axis, count, rank, acc, full, boxes, send, recv):
        self.axis, self.acc, self.full, self.boxes = axis, acc, full, boxes
        self.send, self.recv = send, recv
        me = lax.axis_index(axis)
        offset, size = 0, rank
        self.stages = []
        for bit in range(count.bit_length() - 1):
            one = lax.rem(me // (1 << bit), 2)
            peer = me + (1 - 2 * one) * (1 << bit)
            halve = size >= 16
            if halve:
                half = size // 2
                keep, give = offset + one * half, offset + (1 - one) * half
            else:
                half, keep, give = size, offset, offset
            self.stages.append((peer, halve, half, keep, give))
            offset, size = keep, half
        self.offset, self.size = offset, size
        self.back = [s for s in reversed(range(len(self.stages))) if self.stages[s][1]]
        self.steps = len(self.stages) + len(self.back)

    def rows(self, start, size):
        return pl.ds(start if isinstance(start, int) else pl.multiple_of(start, 8), size)

    def copy(self, step, block, cols):
        n = len(self.stages)
        if step < n:
            peer, halve, half, keep, give = self.stages[step]
            src = self.acc.at[self.rows(give, half), cols]
            dst = self.boxes[step].at[:, cols]
        else:
            peer, halve, half, keep, give = self.stages[self.back[step - n]]
            src = self.full.at[self.rows(keep, half), cols]
            dst = self.full.at[self.rows(keep, half), cols]
        return pltpu.make_async_remote_copy(
            src_ref=src,
            dst_ref=dst,
            send_sem=self.send.at[step, block],
            recv_sem=self.recv.at[step, block],
            device_id={self.axis: peer},
            device_id_type=pl.DeviceIdType.MESH,
        )

    def start(self, step, block, cols):
        self.copy(step, block, cols).start()

    def finish(self, step, block, cols):
        self.copy(step, block, cols).wait()
        n = len(self.stages)
        if step < n:
            half, keep = self.stages[step][2:4]
            kept = self.rows(keep, half)
            self.acc[kept, cols] = self.acc[kept, cols] + self.boxes[step][:, cols]
            if step == n - 1:
                own = self.rows(self.offset, self.size)
                self.full[own, cols] = self.acc[own, cols]
        if step + 1 < self.steps:
            self.start(step + 1, block, cols)


def box_rows(count, rank):
    sizes, size = [], rank
    for _ in range(count.bit_length() - 1):
        if size >= 16:
            size //= 2
        sizes.append(size)
    return sizes


def step_count(count, rank):
    size, steps = rank, 0
    for _ in range(count.bit_length() - 1):
        steps += 1
        if size >= 16:
            size //= 2
            steps += 1
    return steps


def factor_kernel(plan, mom, grad, rf, lhs_out, lt_out, rt_out, nt_out, first_out, *refs):
    m, n, rank, nr, nc, tile, chunk, group = plan
    refs = list(refs)
    take = lambda count: [refs.pop(0) for _ in range(count)]
    (bh, bm, mbuf, gbuf, rp, acc, full, yp, ws, lt, first) = take(11)
    boxes_y = take(nc.bit_length() - 1)
    boxes_w = take(nr.bit_length() - 1)
    ex = [take(4) for _ in range(3)]
    (in_sem, out_sem, lhs_sem, ysend, yrecv, wsend, wrecv) = take(7)

    tiles, chunks, per = m // tile, m // chunk, chunk // tile
    pair = min(2, per)
    slots = min(SLOTS, tiles)

    def load(t, slot):
        src = pl.ds(pl.multiple_of(t * tile, tile), tile)
        return (
            pltpu.make_async_copy(mom.at[src, :], mbuf.at[slot], in_sem.at[0, slot]),
            pltpu.make_async_copy(grad.at[src, :], gbuf.at[slot], in_sem.at[1, slot]),
        )

    for t in range(slots):
        for c in load(t, t):
            c.start()

    barrier = pltpu.get_barrier_semaphore()
    row, col = lax.axis_index("row"), lax.axis_index("col")
    for step in range(1, nc):
        pl.semaphore_signal(
            barrier, inc=1, device_id={"col": lax.rem(col + step, nc)}, device_id_type=pl.DeviceIdType.MESH
        )
    for step in range(1, nr):
        pl.semaphore_signal(
            barrier, inc=1, device_id={"row": lax.rem(row + step, nr)}, device_id_type=pl.DeviceIdType.MESH
        )

    r = rf[...]
    r_high, r_rest = halves(r)
    r_mid, r_low = halves(r - r_high.astype(F32))
    pieces = jnp.concatenate([p.astype(F32) for p in (r_high, r_mid, r_low)], axis=0)
    rp[...] = pieces.T.astype(BF16)
    gram_r = dot_high(r, r, ((1,), (1,)))

    pl.semaphore_wait(barrier, nc + nr - 2)

    ex_r = Exchange("col", nc, *ex[0])
    ex_g = Exchange("row", nr, *ex[1])
    ex_s = Exchange("col", nc, *ex[2])
    sum_y = AllReduce("col", nc, rank, acc, full, boxes_y, ysend, yrecv)
    sum_w = AllReduce("row", nr, rank, acc, full, boxes_w, wsend, wrecv)

    ex_r.start(gram_r)

    def chunk_cols(c):
        return pl.ds(pl.multiple_of(c * chunk, chunk), chunk)

    def body(c, carry):
        for step in reversed(range(sum_y.steps)):
            old = c - step - 1

            @pl.when((old >= 0) & (old < chunks))
            def _(step=step, old=old):
                sum_y.finish(step, old, chunk_cols(old))

        @pl.when(c < chunks)
        def _():
            for k in range(0, per, pair):
                for t in range(pair):
                    t = c * per + k + t
                    slot = lax.rem(t, slots)
                    for copy in load(t, slot):
                        copy.wait()
                    high, low = halves(mbuf[slot] + gbuf[slot].astype(F32))
                    here = pl.ds(pl.multiple_of(t * tile, tile), tile)
                    bh[here, :] = high
                    bm[here, :] = low

                    @pl.when(t + slots < tiles)
                    def _(t=t, slot=slot):
                        for copy in load(t + slots, slot):
                            copy.start()

                here = pl.ds(pl.multiple_of((c * per + k) * tile, pair * tile), pair * tile)
                both = jnp.concatenate([bh[here, :], bm[here, :]], axis=0)
                part = dot_bf16(both, rp[...])
                part = (part[: pair * tile] + part[pair * tile :]).T
                acc[:, here] = part[:rank] + (part[rank : 2 * rank] + part[2 * rank :])

            sum_y.start(0, c, chunk_cols(c))

        @pl.when(c == chunks)
        def _():
            g = ex_r.finish()
            rows = lax.broadcasted_iota(jnp.int32, (rank, rank), 0)
            cols = lax.broadcasted_iota(jnp.int32, (rank, rank), 1)
            diag = jnp.where(rows == cols, g, 0.0)
            trace = jnp.sum(jnp.sum(diag, axis=1, keepdims=True), axis=0, keepdims=True)
            ws[...] = widen(g + jnp.where(rows == cols, trace * (2.0**-22), 0.0))

        for k in range(4):

            @pl.when(c == chunks + min(k, sum_y.steps - 1))
            def _(k=k):
                ws[...] = eliminate_columns(ws[...], range(k * rank // 4, (k + 1) * rank // 4))

        return carry

    lax.fori_loop(0, chunks + sum_y.steps, body, 0)
    upper_r, q = split_factors(ws[...])

    def whiten(c, gram):
        cols = chunk_cols(c)
        y = dot_high(q, full[:, cols], ((1,), (0,)))
        lt[:, cols] = y
        high, low = halves(y)
        yp[:rank, cols] = high
        yp[rank:, cols] = low
        return gram + dot_high(y, y, ((1,), (1,)))

    gram_y = lax.fori_loop(0, chunks, whiten, jnp.zeros((rank, rank), F32))
    ex_g.start(gram_y)

    groups = n // group
    sub = min(256, group)

    def group_cols(g):
        return pl.ds(g * group, group)

    def right_part(g):
        def one(s, carry):
            cols = pl.ds(pl.multiple_of(g * group + s * sub, sub), sub)
            w = dot_bf16(yp[...], bh[:, cols]) + dot_bf16(yp[...], bm[:, cols])
            acc[:, cols] = w[:rank] + w[rank:]
            return carry

        lax.fori_loop(0, group // sub, one, 0)
        sum_w.start(0, g, group_cols(g))

    across = n // (4 * rank)

    def lhs_copy(t):
        lanes = pl.ds(pl.multiple_of(lax.rem(t, across) * 4 * rank, 4 * rank), 4 * rank)
        rows = pl.ds(pl.multiple_of(t * tile, tile), tile)
        return pltpu.make_async_copy(gbuf.at[t // across, :, lanes], lhs_out.at[rows, :], lhs_sem.at[t])

    def left_part(t, carry):
        cols = pl.ds(pl.multiple_of(t * tile, tile), tile)
        left_t = dot_high(both, lt[:, cols], ((1,), (0,)))
        lt[:, cols] = left_t
        high = left_t.astype(BF16).astype(F32)
        low = left_t - high
        lanes = pl.ds(pl.multiple_of(lax.rem(t, across) * 4 * rank, 4 * rank), 4 * rank)
        gbuf[t // across, :, lanes] = jnp.concatenate([high, high, low, low], axis=0).T.astype(BF16)
        lhs_copy(t).start()
        return carry

    def lhs_end(t, carry):
        lhs_copy(t).wait()
        return carry

    def out(k, src, dst):
        return pltpu.make_async_copy(src, dst, out_sem.at[k])

    lt_copy = out(0, lt, lt_out)
    rt_copy = out(1, acc.at[:, pl.ds(0, n)], rt_out)
    nt_copy = out(2, full.at[:, pl.ds(0, n)], nt_out)
    first_copy = out(3, first, first_out)

    for i in range(groups + max(sum_w.steps, 3)):
        for step in reversed(range(sum_w.steps)):
            if 0 <= i - 1 - step < groups:
                sum_w.finish(step, i - 1 - step, group_cols(i - 1 - step))
        if i < groups:
            right_part(i)
        if i == groups:
            g_all = ex_g.finish()
            upper, inverse = eliminate(g_all)
            first[...] = dot_high(upper_r, upper, ((0,), (1,))) * (
                1.0 / math.sqrt(float(m * nr) * float(n * nc))
            )
        if i == groups + 1:
            g_two = dot_high(dot_high(inverse, g_all, ((1,), (0,))), inverse, ((1,), (1,)))
            _, inverse_two = eliminate(g_two)
            both = dot_high(inverse_two, inverse, ((1,), (0,)))
        if i == groups + 2:
            lax.fori_loop(0, tiles, left_part, 0)
            lt_copy.start()
            first_copy.start()

    squares = jnp.zeros((rank, 1), F32)
    for g in range(groups):
        right = dot_high(both, full[:, group_cols(g)], ((1,), (0,)))
        acc[:, group_cols(g)] = right
        squares = squares + jnp.sum(right * right, axis=1, keepdims=True)
    rt_copy.start()
    ex_s.start(jnp.broadcast_to(squares, (rank, 128)))
    norms = jnp.sqrt(ex_s.finish()[:, :1]) + 1e-06
    full[:, :n] = acc[:, :n] * (1.0 / norms)
    nt_copy.start()
    lax.fori_loop(0, tiles, lhs_end, 0)
    for copy in (lt_copy, rt_copy, nt_copy, first_copy):
        copy.wait()


def factors(plan, momentum, gradient, right_factor):
    m, n, rank, nr, nc, tile, chunk, group = plan
    slots = min(SLOTS, m // tile)
    vmem = pltpu.VMEM
    dma = pltpu.SemaphoreType.DMA

    def exchange(count, width):
        return [vmem((rank, width), F32), vmem((count, rank, width), F32), dma((count,)), dma((count,))]

    scratch = [
        vmem((m, n), BF16),
        vmem((m, n), BF16),
        vmem((slots, tile, n), F32),
        vmem((slots, tile, n), BF16),
        vmem((n, 3 * rank), BF16),
        vmem((rank, max(m, n)), F32),
        vmem((rank, max(m, n)), F32),
        vmem((2 * rank, m), BF16),
        vmem((rank, 2 * rank), F32),
        vmem((rank, m), F32),
        vmem((rank, rank), F32),
    ]
    scratch += [vmem((rows, m), F32) for rows in box_rows(nc, rank)]
    scratch += [vmem((rows, n), F32) for rows in box_rows(nr, rank)]
    scratch += exchange(nc, rank) + exchange(nr, rank) + exchange(nc, 128)
    steps_y, steps_w = step_count(nc, rank), step_count(nr, rank)
    scratch += [
        dma((2, slots)),
        dma((4,)),
        dma((m // tile,)),
        dma((steps_y, m // chunk)),
        dma((steps_y, m // chunk)),
        dma((steps_w, n // group)),
        dma((steps_w, n // group)),
    ]
    whole = pl.BlockSpec(memory_space=vmem)
    return pl.pallas_call(
        functools.partial(factor_kernel, plan),
        out_shape=[
            jax.ShapeDtypeStruct((m, 4 * rank), BF16),
            jax.ShapeDtypeStruct((rank, m), F32),
            jax.ShapeDtypeStruct((rank, n), F32),
            jax.ShapeDtypeStruct((rank, n), F32),
            jax.ShapeDtypeStruct((rank, rank), F32),
        ],
        in_specs=[pl.BlockSpec(memory_space=pl.ANY), pl.BlockSpec(memory_space=pl.ANY), whole],
        out_specs=[pl.BlockSpec(memory_space=pl.ANY)] * 5,
        scratch_shapes=scratch,
        compiler_params=pltpu.CompilerParams(
            collective_id=0, has_side_effects=True, vmem_limit_bytes=60 * MIB
        ),
        name="factors",
    )(momentum, gradient, right_factor)


def output_kernel(scale, rank, mom, grad, lhs, lt, rt, nt, first, update, left, normed, new, first_out, rhs_u, rhs_m):
    tile, n = mom.shape

    @pl.when(pl.program_id(0) == 0)
    def _():
        normed[...] = nt[...]
        first_out[...] = first[...]
        for ref, value in ((rhs_u, nt[...] * scale), (rhs_m, rt[...] * 0.05)):
            high, low = halves(value)
            for k in range(2):
                ref[2 * k * rank : (2 * k + 1) * rank, :] = high
                ref[(2 * k + 1) * rank : (2 * k + 2) * rank, :] = low

    left[...] = lt[...]
    rows = lhs[...]
    width = min(256, n)
    for at in range(0, n, width):
        cols = pl.ds(at, width)
        update[:, cols] = dot_bf16(rows, rhs_u[:, cols]).astype(BF16)
        new[:, cols] = (mom[:, cols] + grad[:, cols].astype(F32)) - dot_bf16(rows, rhs_m[:, cols])


def outputs(scale, tile, momentum, gradient, lhs, lt, rt, nt, first):
    m, n = momentum.shape
    rank = lt.shape[0]
    fixed = lambda shape: pl.BlockSpec(shape, lambda i: (0, 0))
    rows = lambda width: pl.BlockSpec((tile, width), lambda i: (i, 0))
    return pl.pallas_call(
        functools.partial(output_kernel, scale, rank),
        grid=(m // tile,),
        out_shape=[
            jax.ShapeDtypeStruct((m, n), BF16),
            jax.ShapeDtypeStruct((rank, m), F32),
            jax.ShapeDtypeStruct((rank, n), F32),
            jax.ShapeDtypeStruct((m, n), F32),
            jax.ShapeDtypeStruct((rank, rank), F32),
        ],
        in_specs=[
            rows(n),
            rows(n),
            rows(4 * rank),
            pl.BlockSpec((rank, tile), lambda i: (0, i)),
            fixed((rank, n)),
            fixed((rank, n)),
            fixed((rank, rank)),
        ],
        out_specs=[
            rows(n),
            pl.BlockSpec((rank, tile), lambda i: (0, i)),
            fixed((rank, n)),
            rows(n),
            fixed((rank, rank)),
        ],
        scratch_shapes=[pltpu.VMEM((4 * rank, n), BF16), pltpu.VMEM((4 * rank, n), BF16)],
        compiler_params=pltpu.CompilerParams(vmem_limit_bytes=60 * MIB),
        name="outputs",
    )(momentum, gradient, lhs, lt, rt, nt, first)


def on_device(nr, nc, momentum, gradient, right_factor):
    m, n = momentum.shape
    rank = right_factor.shape[1]
    tile = min(128, m)
    chunk = min(512, m)
    group = min(512, n)
    plan = (m, n, rank, nr, nc, tile, chunk, group)
    scale = math.sqrt(float(m * nr) * float(n * nc) / float(rank))
    lhs, lt, rt, nt, first = factors(plan, momentum, gradient, right_factor.T)
    update, left, normed, new, first = outputs(
        scale, min(512, m), momentum, gradient, lhs, lt, rt, nt, first
    )
    return update, left.T, normed.T, new, first


def solution(mesh):
    in_specs = (P("row", "col"), P("row", "col"), P("col", None))
    out_specs = (P("row", "col"), P("row", None), P("col", None), P("row", "col"), P())
    return jax.shard_map(
        functools.partial(on_device, mesh.shape["row"], mesh.shape["col"]),
        mesh=mesh,
        in_specs=in_specs,
        out_specs=out_specs,
        check_vma=False,
    )
```
